128 devices in a mesh: dp: 64 (over x, z_lo, y, core), tensor: 2 (over z_hi).
Axes of the slice: x: 4, y: 4, z: 4 (z_hi: 2, z_lo: 2; z = z_hi * 2 + z_lo), core: 2. Of those that a mesh axis runs over, the one named last changes fastest.
Arguments:
- images: bfloat16 [128, 197, 768], P('dp'), may hold values from -6 to 6
- counts: int32 [64], P('dp'), may hold values from 1 to 2, as said below
- ln1_gain: bfloat16 [768], replicated, may hold values from 0.099609375 to 1.8984375
- ln1_bias: bfloat16 [768], replicated, may hold values from -3 to 3
- qkv_weight: bfloat16 [3, 768, 768], P(None, None, 'tensor'), may hold values from -0.21875 to 0.21875
- qv_bias: bfloat16 [2, 768], P(None, 'tensor'), may hold values from -3 to 3
- proj_weight: bfloat16 [768, 768], P('tensor'), may hold values from -0.625 to 0.625
- proj_bias: bfloat16 [768], replicated, may hold values from -3 to 3
- ln2_gain: bfloat16 [768], replicated, may hold values from 0.099609375 to 1.8984375
- ln2_bias: bfloat16 [768], replicated, may hold values from -3 to 3
- fc1_weight: bfloat16 [768, 3072], P(None, 'tensor'), may hold values from -0.21875 to 0.21875
- fc1_bias: bfloat16 [3072], P('tensor'), may hold values from -3 to 3
- fc2_weight: bfloat16 [3072, 768], P('tensor'), may hold values from -0.109375 to 0.109375
- fc2_bias: bfloat16 [768], replicated, may hold values from -3 to 3
- cotangent: bfloat16 [128, 197, 768], P('dp'), may hold values from -6 to 6
Outputs:
- block_out: float32 [128, 197, 768], P('dp')
- grad_images: float32 [128, 197, 768], P('dp')
- grad_ln1_gain: float32 [768], replicated
- grad_ln1_bias: float32 [768], replicated
- grad_qkv: float32 [3, 768, 768], P(None, None, 'tensor')
- grad_qv_bias: float32 [2, 768], P(None, 'tensor')
- grad_proj: float32 [768, 768], P('tensor')
- grad_proj_bias: float32 [768], replicated
- grad_ln2_gain: float32 [768], replicated
- grad_ln2_bias: float32 [768], replicated
- grad_fc1: float32 [768, 3072], P(None, 'tensor')
- grad_fc1_bias: float32 [3072], P('tensor')
- grad_fc2: float32 [3072, 768], P('tensor')
- grad_fc2_bias: float32 [768], replicated
The draws below stay inside these ranges and needn't reach their ends.
Inputs may be any that keep to these rules, and one draw needn't show every extreme that they name: `counts`: every index of dp holds its live images in its first slots; some index holds 2 and some holds 1.
All inputs are finite; a program needn't handle non-finite values.
Results may differ from the reference program's by a relative error of at most 0.012.
The reference program's roundings to bfloat16 on the way count: a program that leaves them out, or rounds other values in their place, can miss the bound.
Values sent between devices are 32-bit elements; how exact they have to be, the bound alone decides.
No kernel may reach another device: no remote copies, remote signals or barrier semaphores. Data moves between devices by JAX's collectives and lax.ppermute only.
A program may use at most 128 MiB of HBM per device.

```python
import jax
import jax.numpy as jnp
from jax import lax

D = 768
HEADS = 12
FF = 3072
SEQ = 197
IMG_CAP = 2
N_IMG = 128
N_DP = 64


def draw_counts(key, part):
    key = jax.random.fold_in(key, 7)
    first_key, second_key = jax.random.split(key)
    drawn = jax.random.randint(first_key, (N_DP,), 1, IMG_CAP + 1)
    order = jax.random.permutation(second_key, N_DP)
    drawn = drawn.at[order[0]].set(IMG_CAP)
    drawn = drawn.at[order[1]].set(1)
    return drawn.astype(jnp.int32)


def levels(own_key, dims, pieces, low, top_value):
    gain = 1.0
    for dim, shards_of in pieces:
        draws = jax.random.uniform(jax.random.fold_in(jax.random.fold_in(own_key, 6), dim), (shards_of,), jnp.float32, low / len(pieces), top_value / len(pieces))
        gain = gain * jnp.repeat(jnp.exp(draws), dims[dim] // shards_of).reshape((-1,) + (1,) * (len(dims) - 1 - dim))
    return gain


def noise(rng, dims, width, bound, pieces=(), kind=jnp.bfloat16):
    values = jax.random.normal(rng, dims, jnp.float32) * width
    if len(pieces) > 0:
        values = levels(rng, dims, pieces, -0.22, 0.18) * values
    return jnp.clip(values, min=-bound, max=bound).astype(kind)


def setup_inputs(seed: int = 0) -> dict:
    key_of = jax.random.split(jax.random.key(seed), 16)
    return {
        "images": noise(key_of[0], (N_IMG, SEQ, D), 1.0, 6.0, ((0, 64),)),
        "counts": draw_counts(jax.random.fold_in(key_of[15], 71), 0),
        "ln1_gain": jnp.clip(1.0 + 0.18 * jax.random.normal(key_of[2], (D,), jnp.float32), 0.099609375, 1.8984375).astype(jnp.bfloat16),
        "ln1_bias": noise(key_of[3], (D,), 0.5, 3.0),
        "qkv_weight": noise(key_of[4], (3, D, D), D ** -0.5, 0.21875, ((2, 2),)),
        "qv_bias": noise(key_of[5], (2, D), 0.5, 3.0, ((1, 2),)),
        "proj_weight": noise(key_of[6], (D, D), (D // 8) ** -0.5, 0.625, ((0, 2),)),
        "proj_bias": noise(key_of[7], (D,), 0.5, 3.0),
        "ln2_gain": jnp.clip(1.0 + 0.18 * jax.random.normal(key_of[8], (D,), jnp.float32), 0.099609375, 1.8984375).astype(jnp.bfloat16),
        "ln2_bias": noise(key_of[9], (D,), 0.5, 3.0),
        "fc1_weight": noise(key_of[10], (D, FF), D ** -0.5, 0.21875, ((1, 2),)),
        "fc1_bias": noise(key_of[11], (FF,), 0.5, 3.0, ((0, 2),)),
        "fc2_weight": noise(key_of[12], (FF, D), FF ** -0.5, 0.109375, ((0, 2),)),
        "fc2_bias": noise(key_of[13], (D,), 0.5, 3.0),
        "cotangent": noise(key_of[14], (N_IMG, SEQ, D), 1.0, 6.0, ((0, 64),)),
    }


@jax.custom_vjp
def low(v):
    return lax.optimization_barrier(v.astype(jnp.bfloat16)).astype(jnp.float32)

@jax.custom_vjp
def low_back(v):
    return v

def low_keep(v):
    return (low(v), None)

def low_pass(kept, grad):
    return (grad,)

def back_keep(v):
    return (v, None)

def back_low(kept, grad):
    return (low(grad),)
low.defvjp(low_keep, low_pass)
low_back.defvjp(back_keep, back_low)
EPSILON = 1e-06
HIGHEST = lax.Precision.HIGHEST

def layer_norm(values, scale_gain, offset):
    average = lax.optimization_barrier(jnp.mean(values, axis=-1, keepdims=True))
    centred = values - average
    variance = lax.optimization_barrier(jnp.mean(centred * centred, axis=-1, keepdims=True))
    return centred * lax.rsqrt(variance + EPSILON) * scale_gain + offset

def block_forward(weights, pictures, alive_mask):
    ln1_gain, ln1_bias, qkv_weight, qv_bias, proj_weight, proj_bias, ln2_gain, ln2_bias, fc1_weight, fc1_bias, fc2_weight, fc2_bias = weights
    images_here, length, model_width = pictures.shape
    head_size = model_width // HEADS
    scale = float(head_size) ** (-0.5)
    flat_rows = pictures.reshape(images_here * length, model_width)
    normed_one = low(layer_norm(flat_rows, ln1_gain, ln1_bias))
    projected = jnp.einsum('td,cde->cte', normed_one, qkv_weight, precision=HIGHEST)
    shape_heads = (images_here, length, HEADS, head_size)
    queries = low(low_back(projected[0] + qv_bias[0])).reshape(shape_heads)
    keys_all = low(low_back(projected[1])).reshape(shape_heads)
    values_all = low(low_back(projected[2] + qv_bias[1])).reshape(shape_heads)
    scores = low_back(jnp.einsum('bqhd,bkhd->bhqk', queries, keys_all, precision=HIGHEST)) * scale
    soft_low = low(jax.nn.softmax(scores, axis=-1))
    mixed_heads = jnp.einsum('bhqk,bkhd->bqhd', soft_low, values_all, precision=HIGHEST)
    mixed_low = low(low_back(mixed_heads.reshape(flat_rows.shape[0], model_width)))
    branch_one = low_back(jnp.dot(mixed_low, proj_weight, precision=HIGHEST) + proj_bias)
    middle = flat_rows + branch_one
    normed_two = low(layer_norm(middle, ln2_gain, ln2_bias))
    hidden_pre = low_back(jnp.dot(normed_two, fc1_weight, precision=HIGHEST) + fc1_bias)
    hidden_low = low(jax.nn.gelu(hidden_pre, approximate=False))
    branch_two = low_back(jnp.dot(hidden_low, fc2_weight, precision=HIGHEST) + fc2_bias)
    result = (middle + branch_two).reshape(pictures.shape)
    return result * alive_mask[:, None, None]

def reference(images, counts, ln1_gain, ln1_bias, qkv_weight, qv_bias, proj_weight, proj_bias, ln2_gain, ln2_bias, fc1_weight, fc1_bias, fc2_weight, fc2_bias, cotangent):
    weights = tuple((argument.astype(jnp.float32) for argument in (ln1_gain, ln1_bias, qkv_weight, qv_bias, proj_weight, proj_bias, ln2_gain, ln2_bias, fc1_weight, fc1_bias, fc2_weight, fc2_bias)))
    pictures = images.astype(jnp.float32).reshape(N_DP, IMG_CAP, SEQ, D)
    cotangents = cotangent.astype(jnp.float32).reshape(N_DP, IMG_CAP, SEQ, D)
    slot_index = jnp.arange(IMG_CAP, dtype=jnp.int32)

    def scan_step(summed, inputs):
        group_images, held_count, seed_grad = inputs
        alive_mask = (slot_index < held_count).astype(jnp.float32)
        output, backward = jax.vjp(lambda params, pictures_in: block_forward(params, pictures_in, alive_mask), weights, group_images)
        grad_weights, grad_group = backward(seed_grad)
        summed = jax.tree.map(lambda first_term, second_term: first_term + second_term, summed, grad_weights)
        return (summed, (output, grad_group))
    zero_grads = jax.tree.map(jnp.zeros_like, weights)
    summed, (outputs, grad_pictures) = lax.scan(scan_step, zero_grads, (pictures, counts, cotangents))
    shape_all = (N_IMG, SEQ, D)
    return (outputs.reshape(shape_all), grad_pictures.reshape(shape_all), summed[0], summed[1], summed[2], summed[3], summed[4], summed[5], summed[6], summed[7], summed[8], summed[9], summed[10], summed[11])
```

```python
import functools

import jax
import jax.numpy as jnp
from jax import lax
from jax.experimental import pallas as pl
from jax.experimental.pallas import tpu as pltpu
from jax.sharding import Mesh, PartitionSpec as P

HEADS = 12
SIDE = 4
PLANE = ("x", "y", "core")
DIAGONAL = [(0, 3), (1, 2), (2, 1), (3, 0)]
SWAP = [(0, 1), (1, 0)]


EPSILON = 1e-06


PAD = 200
HEAD = 64
PAIR = 2 * HEAD
STEP = 256
F32 = jnp.float32
BF16 = jnp.bfloat16


def mul(a, b, dims=((1,), (0,))):
    return lax.dot_general(a, b, (dims, ((), ())), preferred_element_type=F32)


ROWS = ((0,), (0,))
COLUMNS = ((1,), (1,))


def normalise(values):
    centred = values - jnp.mean(values, axis=-1, keepdims=True)
    inverse = lax.rsqrt(jnp.mean(centred * centred, axis=-1, keepdims=True) + EPSILON)
    return (centred * inverse, inverse)


def norm_backward(grad_output, normed, inverse, scale_gain):
    grad_normed = grad_output * scale_gain
    first_mean = jnp.mean(grad_normed, axis=-1, keepdims=True)
    second_mean = jnp.mean(grad_normed * normed, axis=-1, keepdims=True)
    return inverse * (grad_normed - first_mean - normed * second_mean)


def column_sum(values):
    return jnp.sum(values, axis=0, keepdims=True)


def soft_of(queries, keys, length):
    scores = mul(queries, keys, COLUMNS) * (float(HEAD) ** -0.5)
    lanes = lax.broadcasted_iota(jnp.int32, scores.shape, 1)
    scores = jnp.where(lanes < length, scores, -1e30)
    expos = jnp.exp(scores - jnp.max(scores, axis=-1, keepdims=True))
    return expos / jnp.sum(expos, axis=-1, keepdims=True)


def image_rows(i):
    return slice(i * PAD, (i + 1) * PAD)


def attend_kernel(length, x, gain, offset, w, qv_bias, proj, first_low, qkv, mixed, *partials):
    normed, _ = normalise(jnp.concatenate([x[i] for i in range(x.shape[0])], axis=0))
    normed = normed * gain[...] + offset[...]
    for i in range(x.shape[0]):
        first_low[i] = normed[image_rows(i)].astype(BF16)
    low = normed.astype(BF16)
    width = proj.shape[0]
    bias = (qv_bias[0:1, :], None, qv_bias[1:2, :])
    parts = []
    for c in range(3):
        part = mul(low, w[c])
        if bias[c] is not None:
            part = part + bias[c]
        part = part.astype(BF16).astype(F32)
        qkv[:, c * width : (c + 1) * width] = part
        parts.append(part)
    lanes = lax.broadcasted_iota(jnp.int32, (PAD, PAIR), 1)
    for i in range(x.shape[0]):
        for p in range(width // PAIR):
            cols = slice(p * PAIR, (p + 1) * PAIR)
            queries, keys, values = (part[image_rows(i), cols] for part in parts)
            keys, values = keys.astype(BF16), values.astype(BF16)
            outs = []
            for h in range(2):
                own = lanes // HEAD == h
                soft = soft_of(jnp.where(own, queries, 0.0).astype(BF16), keys, length)
                outs.append(mul(soft.astype(BF16), values))
            mixed[i, :, cols] = jnp.where(lanes < HEAD, outs[0], outs[1]).astype(BF16)
        partials[i][...] = mul(mixed[i], proj[...])


def half_of(ref, which, index=None):
    half = ref.shape[-1] // 2
    lanes = pl.ds(pl.multiple_of(which * half, 128), half)
    return ref[:, lanes] if index is None else ref[index, :, lanes]


def hidden_kernel(
    image, x, mine, theirs, proj_bias, gain, offset, fc1, fc1_bias, fc2, gout, *refs
):
    middle, second_low, hidden_low, dpre_low, partial_two, partial_three, dbias, dnorm = refs[-8:]
    mid = x[image] + (mine[...] + theirs[...] + proj_bias[...])
    middle[...] = mid
    normed, _ = normalise(mid)
    low = (normed * gain[...] + offset[...]).astype(BF16)
    second_low[...] = low
    grads = gout[image]
    out, back = None, None
    for j in range(fc1.shape[1] // STEP):
        cols = slice(j * STEP, (j + 1) * STEP)
        pre = mul(low, fc1[:, cols]) + fc1_bias[:, cols]
        below = 0.5 * (1.0 + lax.erf(pre * (0.5**0.5)))
        density = jnp.exp(-0.5 * pre * pre) * 0.3989422804014327
        hidden = (pre * below).astype(BF16)
        hidden_low[:, cols] = hidden
        grad = mul(grads, fc2[cols, :], COLUMNS)
        dpre = ((below + pre * density) * grad).astype(BF16)
        dpre_low[:, cols] = dpre
        dbias[:, cols] = column_sum(dpre.astype(F32))
        forward = mul(hidden, fc2[cols, :])
        backward = mul(dpre, fc1[:, cols], COLUMNS)
        out = forward if out is None else out + forward
        back = backward if back is None else back + backward
    partial_two[...] = out
    partial_three[...] = back
    dnorm[0:1, :] = column_sum(back * normed)
    dnorm[1:2, :] = column_sum(back)
    if len(refs) > 8:
        core, second_before, hidden_before, dpre_before, *products = refs[:-8]
        for which, fc2_product, fc1_product in (
            (1 - core[0], products[0], products[1]),
            (core[0], products[2], products[3]),
        ):
            fc2_product[...] = mul(half_of(hidden_before, which), gout[1 - image], ROWS) + mul(
                half_of(hidden_low, which), grads, ROWS
            )
            fc1_product[...] = mul(half_of(second_before, which), dpre_before[...], ROWS) + mul(
                half_of(second_low, which), dpre_low[...], ROWS
            )


def attend_back_kernel(
    length, image, x, middle, mine, theirs, gout, gain_two, proj, qkv, w, *refs
):
    last_call = len(refs) > 7
    dmiddle, gmid_low, dqkv, partial, dnorm, dproj_bias, dqv_bias = refs[14:21] if last_call else refs
    normed, inverse = normalise(middle[...])
    dmid = gout[image].astype(F32) + norm_backward(
        mine[...] + theirs[...], normed, inverse, gain_two[...]
    )
    dmiddle[...] = dmid
    low = dmid.astype(BF16)
    gmid_low[...] = low
    dproj_bias[...] = column_sum(low.astype(F32))
    dmixed = mul(low, proj[...], COLUMNS).astype(BF16).astype(F32)
    width = proj.shape[0]
    lanes = lax.broadcasted_iota(jnp.int32, (PAD, PAIR), 1)
    for p in range(width // PAIR):
        queries, keys, values = (
            qkv[image_rows(image), c * width + p * PAIR : c * width + (p + 1) * PAIR]
            for c in range(3)
        )
        grads = dmixed[:, p * PAIR : (p + 1) * PAIR]
        queries_low, keys_low = queries.astype(BF16), keys.astype(BF16)
        values_low, grads_low = values.astype(BF16), grads.astype(BF16)
        pieces = ([], [], [])
        for h in range(2):
            own = lanes // HEAD == h
            soft = soft_of(jnp.where(own, queries, 0.0).astype(BF16), keys_low, length)
            dsoft = mul(jnp.where(own, grads, 0.0).astype(BF16), values_low, COLUMNS)
            inner = jnp.sum(dsoft * soft, axis=-1, keepdims=True)
            dscores = (soft * (dsoft - inner) * (float(HEAD) ** -0.5)).astype(BF16)
            pieces[0].append(mul(dscores, keys_low))
            pieces[1].append(mul(dscores, queries_low, ROWS))
            pieces[2].append(mul(soft.astype(BF16), grads_low, ROWS))
        for c in range(3):
            cols = slice(c * width + p * PAIR, c * width + (p + 1) * PAIR)
            dqkv[:, cols] = jnp.where(lanes < HEAD, pieces[c][0], pieces[c][1]).astype(BF16)
    out = None
    for c in range(3):
        part = dqkv[:, c * width : (c + 1) * width]
        if c != 1:
            dqv_bias[:, c // 2 * width : (c // 2 + 1) * width] = column_sum(part.astype(F32))
        product = mul(part, w[c], COLUMNS)
        out = product if out is None else out + product
    partial[...] = out
    normed_one, _ = normalise(x[image])
    dnorm[0:1, :] = column_sum(out * normed_one)
    dnorm[1:2, :] = column_sum(out)
    if last_call:
        (
            core, first_low, mixed, gmid_before, dqkv_before, dnorm_before, dproj_before, dqv_before,
            dnorm_two_before, dnorm_two, dbias_before, dbias, last_theirs, last_mine,
        ) = refs[:14]
        vectors, turned = refs[21:]
        model_width = x.shape[2]
        vectors[...] = jnp.zeros_like(vectors)
        vectors[0:2, :] = dnorm[...] + dnorm_before[...]
        vectors[2:4, :] = dnorm_two[...] + dnorm_two_before[...]
        vectors[4:5, :] = dproj_bias[...] + dproj_before[...]
        vectors[5:6, :] = column_sum(gout[0].astype(F32)) + column_sum(gout[1].astype(F32))
        dbias_all = dbias[...] + dbias_before[...]
        vectors[6:7, :] = dbias_all[:, :model_width]
        vectors[7:8, :] = dbias_all[:, model_width:]
        vectors[8:9, :] = dqv_bias[...] + dqv_before[...]
        turned[...] = vectors[...].T
        half = model_width // 2
        for which, last in ((1 - core[0], last_theirs), (core[0], last_mine)):
            product = mul(half_of(first_low, which, 0), dqkv_before[...], ROWS) + mul(
                half_of(first_low, which, 1), dqkv[...], ROWS
            )
            last[:, :width] = product[:, :width]
            last[:, 2 * width + 128 :] = product[:, width:]
            last[:, width : 2 * width] = mul(half_of(gmid_before, which), mixed[0], ROWS) + mul(
                half_of(gmid_low, which), mixed[1], ROWS
            )
            last[:, 2 * width : 2 * width + 128] = turned[
                pl.ds(pl.multiple_of(which * half, 8), half), :
            ]


def place_kernel(part, fc2, fc1, qkv, proj, fc1_bias, qv_bias, *refs):
    vectors, proj_rows, vector_rows = refs[:-2], refs[-2], refs[-1]
    group = part.shape[0]
    width = fc2.shape[1]
    half = width // 2
    first, second = fc2.shape[0] // group, fc1.shape[0] // group
    one = first + fc1.shape[1] // width * second
    base = (pl.program_id(0) * pl.num_programs(1) + pl.program_id(1)) * (group * second)
    for g in range(group):
        here = part.at[g, 0]
        rows = slice(g * second, (g + 1) * second)
        fc2[g * first : (g + 1) * first, :] = here[:first, :]
        for i in range(fc1.shape[1] // width):
            start = first + i * second
            fc1[rows, i * width : (i + 1) * width] = here[start : start + second, :]
        qkv[0, rows, :] = here[one : one + second, :half]
        for c in (1, 2):
            qkv[c, rows, :] = here[one + second : one + 2 * second, (c - 1) * half : c * half]
        start = pl.multiple_of(base + g * second, 8)
        proj_rows[pl.ds(start, second), :] = here[one : one + second, half:]
        for k in range(second // 8):
            packed = here[one + 2 * second :, k * 128 : (k + 1) * 128]
            vector_rows[pl.ds(pl.multiple_of(start + 8 * k, 8), 8), :] = packed

    @pl.when((pl.program_id(0) == 1) & (pl.program_id(1) == pl.num_programs(1) - 1))
    def finish():
        proj[...] = proj_rows[...].T
        turned = vector_rows[...].T
        for k, vector in enumerate(vectors):
            vector[...] = turned[k, :]
        fc1_bias[:width] = turned[6, :]
        fc1_bias[width:] = turned[7, :]
        qv_bias[0:1, :] = turned[8:9, :half]
        qv_bias[1:2, :] = turned[8:9, half:]


def place(parts, hidden_units):
    count, rows, width = parts.shape
    group = 4
    half = width // 2
    steps = count // 2 // group
    small = half // steps
    parts = parts.reshape(count // 2, 2, rows, width)

    def target(c, i):
        return (c * steps + i, 0)

    whole = pl.BlockSpec(memory_space=pltpu.VMEM)
    return pl.pallas_call(
        place_kernel,
        grid=(2, steps),
        out_shape=(
            shape(F32, hidden_units, width),
            shape(F32, width, hidden_units),
            shape(F32, 3, width, half),
            shape(F32, half, width),
            shape(F32, hidden_units),
            shape(F32, 2, half),
        )
        + (shape(F32, width),) * 6,
        in_specs=[pl.BlockSpec((group, 1, rows, width), lambda c, i: (i, c, 0, 0))],
        out_specs=(
            pl.BlockSpec((hidden_units // 2 // steps, width), target),
            pl.BlockSpec((small, hidden_units), target),
            pl.BlockSpec((3, small, half), lambda c, i: (0, c * steps + i, 0)),
        )
        + (whole,) * 9,
        scratch_shapes=[pltpu.VMEM((width, half), F32), pltpu.VMEM((width, 128), F32)],
        compiler_params=pltpu.CompilerParams(vmem_limit_bytes=56 * 2**20),
        cost_estimate=pl.CostEstimate(flops=0, bytes_accessed=8 * parts.size, transcendentals=0),
    )(parts)


def call(kernel, outs, mib, flops, *operands, scratch=()):
    moved = sum(a.size * a.dtype.itemsize for a in (*operands, *outs))
    whole = pl.BlockSpec(memory_space=pltpu.VMEM)
    scalar = pl.BlockSpec(memory_space=pltpu.SMEM)
    return pl.pallas_call(
        kernel,
        out_shape=outs,
        in_specs=[scalar if a.dtype == jnp.int32 else whole for a in operands],
        out_specs=[whole] * len(outs),
        scratch_shapes=list(scratch),
        compiler_params=pltpu.CompilerParams(vmem_limit_bytes=mib * 2**20),
        cost_estimate=pl.CostEstimate(flops=flops, bytes_accessed=moved, transcendentals=0),
    )(*operands)


def shape(dtype, *dims):
    return jax.ShapeDtypeStruct(dims, dtype)


def tensor_other(partial):
    return lax.ppermute(partial, "tensor", SWAP)


def shifted(values, axis, step):
    return lax.ppermute(values, axis, [(i, (i + step) % SIDE) for i in range(SIDE)])


def places_of(axis):
    place = lax.axis_index(axis)
    return tuple((place + step) & (SIDE - 1) for step in range(SIDE))


def pick(blocks, places, dim, step):
    starts = [0] * blocks.ndim
    starts[dim] = places[step]
    sizes = list(blocks.shape)
    sizes[dim] = 1
    taken = lax.dynamic_slice(blocks, starts, sizes, allow_negative_indices=False)
    return lax.squeeze(taken, (dim,))


def ring_scatter(blocks, axis, places, dim=0):
    parts = [pick(blocks, places[axis], dim, step) for step in range(SIDE)]
    moved = [shifted(parts[step], axis, step) for step in (1, 2, 3)]
    return (parts[0] + moved[1]) + (moved[0] + moved[2])


def two_way_first(blocks, axis, places, dim=0):
    cut = blocks.shape[-1] // 2
    own, up, far, down = (pick(blocks, places[axis], dim, step) for step in range(SIDE))
    above = shifted(jnp.concatenate((far[..., :cut], up[..., cut:]), axis=-1), axis, 1)
    below = shifted(jnp.concatenate((down[..., :cut], far[..., cut:]), axis=-1), axis, 3)
    return (own, above, below, up[..., :cut] + above[..., :cut], down[..., cut:] + below[..., cut:])


def two_way_second(state, axis):
    own, above, below, up, down = state
    return (own, above, below, shifted(up, axis, 1), shifted(down, axis, 3))


def two_way_sum(state):
    own, above, below, up, down = state
    cut = up.shape[-1]
    first = own[..., :cut] + below[..., :cut] + up
    second = own[..., cut:] + above[..., cut:] + down
    return jnp.concatenate((first, second), axis=-1)


def joined_columns(values, count):
    width = values.shape[-1] // count
    return jnp.concatenate([values[..., i * width : (i + 1) * width] for i in range(count)], axis=-2)


def tied(values, others):
    return lax.optimization_barrier((values, others))[0]


def core_sum(theirs, mine):
    return mine + lax.ppermute(theirs, "core", SWAP)


def on_device(
    images,
    counts,
    ln1_gain,
    ln1_bias,
    qkv_weight,
    qv_bias,
    proj_weight,
    proj_bias,
    ln2_gain,
    ln2_bias,
    fc1_weight,
    fc1_bias,
    fc2_weight,
    fc2_bias,
    cotangent,
):
    images_here, length, model_width = images.shape
    local_width = qkv_weight.shape[2]
    hidden_units = fc1_weight.shape[1]
    indices = (places_of("x"), places_of("y"), lax.axis_index("core")[None])
    images, (places_x, places_y, core) = lax.optimization_barrier((images, indices))
    places = {"x": places_x, "y": places_y}
    padding = ((0, 0), (0, PAD - length), (0, 0))
    alive_mask = jnp.arange(images_here, dtype=jnp.int32) < counts[0]
    x = jnp.pad(images.astype(F32), padding)
    gout = jnp.where(alive_mask[:, None, None], jnp.pad(cotangent, padding), 0)

    def row(vector):
        return vector.astype(F32)[None, :]

    macs = PAD * model_width * local_width
    attention = PAD * PAD * local_width
    rows_float = shape(F32, PAD, model_width)
    rows_low = shape(BF16, PAD, model_width)
    first_low, qkv, mixed_low, *partial_one = call(
        functools.partial(attend_kernel, length),
        (
            shape(BF16, images_here, PAD, model_width),
            shape(F32, images_here * PAD, 3 * local_width),
            shape(BF16, images_here, PAD, local_width),
            rows_float,
            rows_float,
        ),
        16,
        16 * macs + 16 * attention,
        x,
        row(ln1_gain),
        row(ln1_bias),
        qkv_weight,
        qv_bias.astype(F32),
        proj_weight,
    )
    hidden_outs = (
        rows_float,
        rows_low,
        shape(BF16, PAD, hidden_units),
        shape(BF16, PAD, hidden_units),
        rows_float,
        rows_float,
        shape(F32, 1, hidden_units),
        shape(F32, 2, model_width),
    )

    def hidden_call(image, other, extra, products, flops):
        return call(
            functools.partial(hidden_kernel, image),
            products + hidden_outs,
            28,
            8 * PAD * model_width * hidden_units + flops,
            x,
            partial_one[image],
            other,
            row(proj_bias),
            row(ln2_gain),
            row(ln2_bias),
            fc1_weight,
            row(fc1_bias),
            fc2_weight,
            gout,
            *extra,
        )

    other_first = tensor_other(partial_one[0])
    other_second = tensor_other(tied(partial_one[1], other_first))
    before = hidden_call(0, other_first, (), (), 0)
    middle_0, second_0, hidden_0, dpre_0, two_0, three_0, dbias_0, dnorm_two_0 = before
    other_three_0 = tensor_other(tied(three_0, other_second))
    half_fc2 = shape(F32, hidden_units // 2, model_width)
    half_fc1 = shape(F32, model_width // 2, hidden_units)
    after = hidden_call(
        1,
        other_second,
        (core, second_0, hidden_0, dpre_0),
        (half_fc2, half_fc1, half_fc2, half_fc1),
        8 * PAD * model_width * hidden_units,
    )
    fc2_theirs, fc1_theirs, fc2_mine, fc1_mine = after[:4]
    middle_1, _, _, _, two_1, three_1, dbias_1, dnorm_two_1 = after[4:]
    other_three_1 = tensor_other(tied(three_1, other_three_0))

    fc2_theirs, fc1_theirs = tied((fc2_theirs, fc1_theirs), other_three_0)
    sum_fc2 = core_sum(fc2_theirs, fc2_mine)
    sum_fc1 = core_sum(fc1_theirs, fc1_mine)
    state_fc2 = two_way_first(sum_fc2.reshape(SIDE, -1, model_width), "x", places)
    state_fc1 = two_way_first(sum_fc1.reshape(SIDE, SIDE, -1, hidden_units), "y", places, 1)
    other_three_1 = tied(other_three_1, (sum_fc2, sum_fc1))
    states = (two_way_second(state_fc2, "x"), two_way_second(state_fc1, "y"))

    back_outs = (
        rows_float,
        rows_low,
        shape(BF16, PAD, 3 * local_width),
        rows_float,
        shape(F32, 2, model_width),
        shape(F32, 1, model_width),
        shape(F32, 1, 2 * local_width),
    )

    def back_call(image, middle, mine, theirs, extra, products, flops, scratch=()):
        return call(
            functools.partial(attend_back_kernel, length, image),
            products + back_outs,
            22,
            8 * macs + 20 * attention + flops,
            x,
            middle,
            mine,
            theirs,
            gout,
            row(ln2_gain),
            proj_weight,
            qkv,
            qkv_weight,
            *extra,
            scratch=scratch,
        )

    dmiddle_0, gmid_0, dqkv_0, four_0, dnorm_0, dproj_0, dqv_0 = back_call(
        0, middle_0, three_0, other_three_0, (), (), 0
    )
    last_width = 4 * local_width + 128
    half_last = shape(F32, model_width // 2, last_width)
    last_theirs, last_mine, dmiddle_1, _, _, four_1, _, grad_proj_bias, _ = back_call(
        1,
        middle_1,
        three_1,
        other_three_1,
        (
            core, first_low, mixed_low, gmid_0, dqkv_0, dnorm_0, dproj_0, dqv_0,
            dnorm_two_0, dnorm_two_1, dbias_0, dbias_1,
        ),
        (half_last, half_last),
        16 * macs,
        (pltpu.VMEM((128, model_width), F32), pltpu.VMEM((model_width, 128), F32)),
    )
    states = tied(states, grad_proj_bias)
    share_fc2, share_fc1 = (two_way_sum(state) for state in states)
    last_theirs = tied(last_theirs, (state_fc2[3:], state_fc1[3:]))
    last = core_sum(last_theirs, last_mine)
    last_one, last_two = last[:, : model_width + 128], last[:, model_width + 128 :]
    quads = (two_0, two_1, four_0, four_1)
    both_others = tensor_other(jnp.stack(quads))

    def unpadded(values):
        return values[:, :length]

    branch_two = jnp.stack(quads[:2]) + both_others[:2] + fc2_bias.astype(F32)
    middle = jnp.stack((middle_0, middle_1))
    block_out = jnp.where(alive_mask[:, None, None], unpadded(middle + branch_two), 0.0)
    grad_first = jnp.stack(quads[2:]) + both_others[2:]
    normed_one, inverse_one = normalise(x)
    grad_images = unpadded(
        jnp.stack((dmiddle_0, dmiddle_1))
        + norm_backward(grad_first, normed_one, inverse_one, ln1_gain.astype(F32))
    )
    share_one = ring_scatter(last_one.reshape(SIDE, -1, last_one.shape[1]), "x", places)
    state_two = two_way_first(last_two.reshape(SIDE, SIDE, -1, model_width), "y", places, 1)
    share_two = two_way_sum(two_way_second(state_two, "y"))

    share_one = share_one.reshape(SIDE, -1, share_one.shape[-1])
    pack = share_one[:, :, model_width:].reshape(SIDE, 3, 8, 128).transpose(0, 2, 1, 3)
    pack = jnp.pad(pack.reshape(SIDE, 8, 3 * 128), ((0, 0), (0, 0), (0, model_width - 3 * 128)))
    along_y = (share_fc2.reshape(SIDE, -1, model_width), pack, share_one[:, :, :model_width])
    along_y = ring_scatter(jnp.concatenate(along_y, axis=1), "y", places)
    along_x = (joined_columns(share_fc1, hidden_units // model_width), share_two)
    along_x = ring_scatter(jnp.concatenate(along_x, axis=1), "x", places)
    rows_fc2 = hidden_units // (2 * SIDE * SIDE)
    share = jnp.concatenate(
        (along_y[:rows_fc2], along_x[:rows_fc2], along_y[rows_fc2 + 8 :], along_x[rows_fc2:]), axis=0
    )
    pack = along_y[rows_fc2 : rows_fc2 + 8]
    across = lax.ppermute(pack, "tensor", SWAP)
    diagonal = lax.ppermute(pack, ("zlo", "tensor"), DIAGONAL)
    share = jnp.concatenate((share, pack), axis=0)
    share = share + lax.ppermute(share, "zlo", SWAP)
    in_both = jnp.arange(model_width, dtype=jnp.int32)[None, :] % 128 < 4
    pack = share[-8:] + jnp.where(in_both, across + diagonal, 0.0)
    share = jnp.concatenate((share[:-8], pack), axis=0)
    parts = lax.all_gather(share, PLANE, axis=0)
    whole_fc2, whole_fc1, whole_qkv, whole_proj, fc1_bias_sum, qv_bias_sum, *rows = place(
        parts, hidden_units
    )
    return (
        block_out,
        grad_images,
        rows[0],
        rows[1],
        whole_qkv,
        qv_bias_sum,
        whole_proj,
        rows[4],
        rows[2],
        rows[3],
        whole_fc1,
        fc1_bias_sum,
        whole_fc2,
        rows[5],
    )


def solution(mesh):
    n_dp = mesh.shape["dp"]
    side = 4
    axes = ("x", "zlo", "y", "core", "tensor")
    torus = Mesh(mesh.devices.reshape(side, n_dp // (2 * side * side), side, 2, 2), axes)
    data = axes[:4]
    placed = (
        P(data, None, None),
        P(data),
        P(),
        P(),
        P(None, None, "tensor"),
        P(None, "tensor"),
        P("tensor", None),
        P(),
        P(),
        P(),
        P(None, "tensor"),
        P("tensor"),
        P("tensor", None),
        P(),
        P(data, None, None),
    )
    return jax.shard_map(
        on_device,
        mesh=torus,
        in_specs=placed,
        out_specs=(
            P(data, None, None),
            P(data, None, None),
            P(),
            P(),
            P(None, None, "tensor"),
            P(None, "tensor"),
            P("tensor", None),
            P(),
            P(),
            P(),
            P(None, "tensor"),
            P("tensor"),
            P("tensor", None),
            P(),
        ),
        check_vma=False,
    )
```
